32 devices in a mesh: rows: 8 (over z, core), cols: 4 (over y, x).
Axes of the slice: x: 2, y: 2, z: 4, core: 2. Of those that a mesh axis runs over, the one named last changes fastest.
Arguments:
- feat_query: bfloat16 [128, 256, 2048], P('rows', 'cols'), may hold values from -30 to 30
- feat_key: bfloat16 [128, 256, 2048], P('rows', 'cols'), may hold values from -30 to 30
- w_hidden: bfloat16 [2048, 2048], replicated, may hold values from -0.125 to 0.125
- w_out: bfloat16 [2048, 256], replicated, may hold values from -0.125 to 0.125
- w_prop: bfloat16 [256, 256], replicated, may hold values from -0.375 to 0.375
- valid_mask: int32 [128, 256], P('rows', 'cols'), may hold values 0 or 1
- neg_shard: int32 [8, 4, 8, 2], P('rows', 'cols'), may hold values from 0 to 7, as said below
- neg_block: int32 [8, 4, 8, 2], P('rows', 'cols'), may hold values from 0 to 7
Outputs:
- loss_map: float32 [128, 256], P('rows', 'cols')
The draws below stay inside these ranges and needn't reach their ends.
Inputs may be any that keep to these rules, and one draw needn't show every extreme that they name: `neg_shard`: among the 16 entries of one tile, no shard number appears more than 2 times, and some shard number appears exactly 2 times.
All inputs are finite; a program needn't handle non-finite values. No bound on the sum of `valid_mask` on one device may be relied on, other than what follows from the above.
Results may differ from the reference program's by a relative error of at most 0.0006.
Values may be sent and summed in bfloat16 or wider, within the bound.
A program may use at most 128 MiB of HBM per device.

```python
import math
import jax
import jax.numpy as jnp
from jax import lax

C = 2048
HID = 2048
P_SIZE = 256
HD = 16
WD = 64
NPER = 2
NH = 128
NW = 256
QB = 8
CAP = 2
N_ROWS = 8
N_COLS = 4


def scene(key):
    base_key = jax.random.fold_in(key, 11)
    common = jax.random.normal(jax.random.fold_in(base_key, 1), (C,), jnp.float32)
    patch_rows = NH // 8
    patch_cols = NW // 8
    strength = jnp.exp(jax.random.uniform(jax.random.fold_in(base_key, 2), (patch_rows, patch_cols), jnp.float32, math.log(0.2), math.log(5.0)))
    region = jax.random.normal(jax.random.fold_in(base_key, 3), (patch_rows, patch_cols, C), jnp.float32)
    field_map = common[None, None, :] + strength[..., None] * region
    return jnp.repeat(jnp.repeat(field_map, 8, axis=0), 8, axis=1)


def jitter_of(key):
    return jax.random.normal(key, (NH, NW, C), jnp.float32)


def draw_feat_query(key, part):
    values = scene(key) + jitter_of(jax.random.fold_in(key, 21))
    return jnp.clip(values, -30.0, 30.0).astype(jnp.bfloat16)


def draw_feat_key(key, part):
    values = scene(key)[:, ::-1] + jitter_of(jax.random.fold_in(key, 22))
    return jnp.clip(values, -30.0, 30.0).astype(jnp.bfloat16)


def requests_of(key):
    base_key = jax.random.fold_in(key, 31)
    slots_total = N_ROWS * CAP
    wanted_count = QB * NPER

    def for_device(device_key):
        shuffled = jax.random.permutation(jax.random.fold_in(device_key, 1), slots_total)
        position = jnp.argsort(shuffled).astype(jnp.int32)
        candidate = jnp.arange(slots_total, dtype=jnp.int32)
        leading = shuffled[0] // CAP
        scores = jnp.where(candidate // CAP == leading, candidate % CAP - CAP, position)
        chosen = jnp.argsort(scores)[:wanted_count].astype(jnp.int32)
        shard_ids = chosen // CAP
        reorder = jax.random.permutation(jax.random.fold_in(device_key, 2), wanted_count)
        shard_ids = shard_ids[reorder]
        block_ids = jax.random.randint(jax.random.fold_in(device_key, 3), (wanted_count,), 0, QB, jnp.int32)
        return (shard_ids, block_ids)
    device_keys = jax.random.split(base_key, N_ROWS * N_COLS)
    shard_ids, block_ids = jax.vmap(for_device)(device_keys)
    return (shard_ids.reshape(N_ROWS, N_COLS, QB, NPER), block_ids.reshape(N_ROWS, N_COLS, QB, NPER))


def draw_neg_shard(key, part):
    return requests_of(key)[0]


def draw_neg_block(key, part):
    return requests_of(key)[1]


def with_ends(values, own_key, low, top_value):
    extent = values.shape
    spot = [jax.random.randint(jax.random.fold_in(own_key, axis), (), 0, extent[axis]) for axis in range(len(extent))]
    values = values.at[tuple(spot)].set(low)
    longest = extent.index(max(extent))
    spot[longest] = (spot[longest] + 1) % extent[longest]
    return values.at[tuple(spot)].set(top_value)


def noise(own_key, dims, deviation, limit, held_as=jnp.bfloat16):
    return jnp.clip(deviation * jax.random.normal(own_key, dims, jnp.float32), -limit, limit).astype(held_as)


def setup_inputs(seed: int = 0) -> dict:
    streams_of = jax.random.split(jax.random.key(seed), 9)
    feat_query = draw_feat_query(jax.random.fold_in(streams_of[8], 71), 0)
    feat_key = draw_feat_key(jax.random.fold_in(streams_of[8], 71), 0)
    w_hidden = noise(streams_of[2], (C, HID), C ** -0.5, 0.125)
    w_out = noise(streams_of[3], (HID, P_SIZE), HID ** -0.5, 0.125)
    w_prop = noise(streams_of[4], (P_SIZE, P_SIZE), P_SIZE ** -0.5, 0.375)
    valid_mask = with_ends((jax.random.randint(streams_of[5], (NH, NW), 0, 8) < 7).astype(jnp.int32), jax.random.fold_in(streams_of[5], 1), 0, 1)
    neg_shard = draw_neg_shard(jax.random.fold_in(streams_of[8], 71), 0)
    neg_block = draw_neg_block(jax.random.fold_in(streams_of[8], 71), 0)
    return dict(feat_query=feat_query, feat_key=feat_key, w_hidden=w_hidden, w_out=w_out, w_prop=w_prop, valid_mask=valid_mask, neg_shard=neg_shard, neg_block=neg_block)


epsilon = 1e-06
sharpness_divisor = 0.1

def normalize(vector):
    return vector * lax.rsqrt(lax.optimization_barrier(jnp.sum(vector * vector, axis=-1, keepdims=True)) + epsilon)

def project(feat_map, w_hidden, w_out):
    rows_all, cols_all, channels = feat_map.shape
    band_stack = feat_map.reshape(N_ROWS, HD * cols_all, channels)

    def one_band(band_rows):
        hidden = jnp.maximum(jnp.dot(band_rows, w_hidden, preferred_element_type=jnp.float32), 0.0).astype(jnp.bfloat16)
        return normalize(jnp.dot(hidden, w_out, preferred_element_type=jnp.float32)).astype(jnp.bfloat16)
    return lax.map(one_band, band_stack).reshape(rows_all, cols_all, -1)

def to_tiles(field_map):
    return field_map.reshape(N_ROWS, HD, N_COLS, WD, -1).transpose(0, 2, 1, 3, 4).reshape(N_ROWS, N_COLS, QB, 128, field_map.shape[-1])

def reference(feat_query, feat_key, w_hidden, w_out, w_prop, valid_mask, neg_shard, neg_block):
    query_map = project(feat_query, w_hidden, w_out)
    target_embedding_lattice = project(feat_key, w_hidden, w_out)
    proj_width = query_map.shape[-1]
    padded = jnp.pad(query_map, ((1, 1), (1, 1), (0, 0)))
    carried = jnp.dot(padded.reshape(-1, proj_width), w_prop, preferred_element_type=jnp.float32).reshape(NH + 2, NW + 2, proj_width)
    centre = query_map.astype(jnp.float32)
    spread = jnp.zeros((NH, NW, proj_width), jnp.float32)
    for row_off in range(3):
        for col_off in range(3):
            beside = padded[row_off:row_off + NH, col_off:col_off + NW].astype(jnp.float32)
            cosine = lax.optimization_barrier(jnp.sum(centre * beside, axis=-1))
            weight = jnp.maximum(cosine, 0.0) ** 2
            spread = spread + weight[..., None] * carried[row_off:row_off + NH, col_off:col_off + NW]
    diffused_pixel_embeddings = normalize(spread).astype(jnp.bfloat16)
    matched_pair_agreement = lax.optimization_barrier(jnp.sum(diffused_pixel_embeddings.astype(jnp.float32) * target_embedding_lattice[:, ::-1].astype(jnp.float32), axis=-1)) / sharpness_divisor
    key_tiles = to_tiles(target_embedding_lattice)
    anchor_patch_lattice = to_tiles(diffused_pixel_embeddings)
    col_ids = jnp.arange(N_COLS, dtype=jnp.int32)[None, :, None, None]
    contrast_pair_agreements = key_tiles[neg_shard, col_ids, neg_block]
    cosine_match_energies = jnp.einsum('irgjp,irgzkp->irgjzk', anchor_patch_lattice.astype(jnp.float32), contrast_pair_agreements.astype(jnp.float32)) / sharpness_divisor
    negsum = lax.optimization_barrier(jnp.sum(jnp.exp(cosine_match_energies), axis=(4, 5)))
    negsum = negsum.reshape(N_ROWS, N_COLS, HD, WD).transpose(0, 2, 1, 3).reshape(NH, NW)
    return valid_mask.astype(jnp.float32) * (jnp.log(jnp.exp(matched_pair_agreement) + negsum) - matched_pair_agreement)
```

```python
import functools

import jax
import jax.numpy as jnp
from jax import lax
from jax.experimental import pallas as pl
from jax.experimental.pallas import tpu as pltpu
from jax.sharding import PartitionSpec as P

EPS = 1e-06
INV_SHARP = 10.0
CHUNK = 256
HOP_LAG = 2
GROUP = 4
BLOCK = 128
F32, BF16 = jnp.float32, jnp.bfloat16
MESH = pl.DeviceIdType.MESH


def normalize(v):
    return v * lax.rsqrt(jnp.sum(v * v, axis=-1, keepdims=True) + EPS)


def dot_t(a, b):
    return lax.dot_general(a, b, (((1,), (1,)), ((), ())), preferred_element_type=F32)


def dot_split(a, b):
    high = a.astype(BF16)
    low = (a - high.astype(F32)).astype(BF16)
    return jnp.dot(high, b, preferred_element_type=F32) + jnp.dot(
        low, b, preferred_element_type=F32
    )


def kernel(
    n_rows, n_cols,
    fq, fk, wh, wo, wp, valid, shard, block, out,
    X, WH, WO, KG, PK, PQ, CF, CB, HB, BAND, PR,
    load, load_w, zr, send_r, send_l, send_s, recv_s, part_s, part_r, halo_s, halo_r,
):
    r, c = lax.axis_index("rows"), lax.axis_index("cols")
    lane, p = lax.rem(r, 2), r // 2
    line = n_rows // 2
    sister = r + 1 - 2 * lane
    height, width = valid.shape
    pixels, per_tile = height * width, height * width // BLOCK
    n_key = pixels // CHUNK
    img = CHUNK // width
    per_chunk = CHUNK // BLOCK
    pitch = PQ.shape[1]

    loads = [pltpu.make_async_copy(wh, WH, load_w.at[0]), pltpu.make_async_copy(wo, WO, load_w.at[1])]
    for k in range(2 * n_key):
        source = fk if k < n_key else fq
        loads.append(
            pltpu.make_async_copy(
                source.at[pl.ds((k % n_key) * CHUNK, CHUNK)], X.at[k], load.at[k]
            )
        )
    for k in (2, 0, 1, *range(3, len(loads))):
        loads[k].start()

    HB[...] = jnp.zeros(HB.shape, BF16)
    PQ[...] = jnp.zeros(PQ.shape, BF16)

    span = (GROUP + 2) * pitch
    shape = (GROUP, width, span)
    a = lax.broadcasted_iota(jnp.int32, shape, 0)
    w = lax.broadcasted_iota(jnp.int32, shape, 1)
    t = lax.broadcasted_iota(jnp.int32, shape, 2)
    down = t // pitch
    j = t - down * pitch
    near = ((j < width) & (j - w <= 1) & (w - j <= 1)) | ((j == width) & (w == width - 1)) | ((j == width + 1) & (w == 0))
    near = near & (down >= a) & (down <= a + 2)
    BAND[...] = jnp.where(near, 1.0, 0.0).astype(F32).reshape(BAND.shape)

    around = [(dr, dc) for dr in (-1, 0, 1) for dc in (-1, 0, 1) if (dr, dc) != (0, 0)]

    def inside(dr, dc):
        return (r + dr >= 0) & (r + dr < n_rows) & (c + dc >= 0) & (c + dc < n_cols)

    barrier = pltpu.get_barrier_semaphore()

    def greet(target):
        pl.semaphore_signal(barrier, inc=1, device_id=target, device_id_type=MESH)

    mirrored = (r, n_cols - 1 - c)
    friends = [(True, (sister, c)), (True, mirrored), (p > 0, (r - 2, c)), (p < line - 1, (r + 2, c))]
    friends += [(inside(dr, dc), (r + dr, c + dc)) for dr, dc in around]
    for there, target in friends:
        if there is True:
            greet(target)
        else:
            pl.when(there)(functools.partial(greet, target))
    met = sum(1 if there is True else there.astype(jnp.int32) for there, _ in friends)
    pl.semaphore_wait(barrier, met)

    def keys_of(q, own, i):
        return KG.at[2 * q + own, pl.ds(i * per_chunk, per_chunk)]

    def copy_z(q, i, right):
        ref = keys_of(q, lane, i)
        return pltpu.make_async_remote_copy(
            src_ref=ref, dst_ref=ref,
            send_sem=(send_r if right else send_l).at[q, i], recv_sem=zr.at[q, i],
            device_id=(r + 2 if right else r - 2, c), device_id_type=MESH,
        )

    def copy_s(q, i, own):
        ref = keys_of(q, own, i)
        return pltpu.make_async_remote_copy(
            src_ref=ref, dst_ref=ref,
            send_sem=send_s.at[q, i], recv_sem=recv_s.at[q, i],
            device_id=(sister, c), device_id_type=MESH,
        )

    def copy_p(i):
        return pltpu.make_async_remote_copy(
            src_ref=keys_of(p, lane, i), dst_ref=PK.at[pl.ds(i * per_chunk, per_chunk)],
            send_sem=part_s.at[i], recv_sem=part_r.at[i],
            device_id=mirrored, device_id_type=MESH,
        )

    def copy_h(dr, dc):
        e = (dr + 1) * 3 + dc + 1
        if dc == 0:
            src = PQ.at[1 if dr < 0 else height, pl.ds(0, width)]
            dst = PQ.at[height + 1 if dr < 0 else 0, pl.ds(0, width)]
        else:
            side = 1 if dc > 0 else 0
            src, dst = CB.at[side], HB.at[1 - side, 1 - dr]
        return pltpu.make_async_remote_copy(
            src_ref=src, dst_ref=dst, send_sem=halo_s.at[e], recv_sem=halo_r.at[e],
            device_id=(r + dr, c + dc), device_id_type=MESH,
        )

    def hop(d, i):
        @pl.when(p - d >= 0)
        def _():
            q = p - d
            copy_z(q, i, True).wait_recv()
            pl.when(p < line - 1)(lambda: copy_z(q, i, True).start())
            copy_s(q, i, lane).start()

        @pl.when(p + d < line)
        def _():
            q = p + d
            copy_z(q, i, False).wait_recv()
            pl.when(p > 0)(lambda: copy_z(q, i, False).start())
            copy_s(q, i, lane).start()

    loads[0].wait()
    loads[1].wait()

    def step(k, carry):
        pltpu.make_async_copy(fk.at[pl.ds(0, CHUNK)], X.at[k], load.at[k]).wait()
        hidden = jnp.maximum(jnp.dot(X[k], WH[...], preferred_element_type=F32), 0.0)
        embedded = normalize(jnp.dot(hidden.astype(BF16), WO[...], preferred_element_type=F32))

        @pl.when(k < n_key)
        def _():
            KG[r, pl.ds(k * per_chunk, per_chunk)] = embedded.astype(BF16).reshape(per_chunk, BLOCK, -1)
            pl.when(p < line - 1)(lambda: copy_z(p, k, True).start())
            pl.when(p > 0)(lambda: copy_z(p, k, False).start())
            copy_s(p, k, lane).start()
            copy_p(k).start()

        @pl.when(k >= n_key)
        def _():
            first = (k - n_key) * img
            lines = embedded.reshape(img, width, -1)
            PQ[pl.ds(first + 1, img), pl.ds(0, width)] = lines.astype(BF16)
            for row in range(img):
                CF[0, pl.ds(first + row, 1)] = lines[row, 0:1]
                CF[1, pl.ds(first + row, 1)] = lines[row, width - 1 : width]

        for d in range(1, line):
            i = k - HOP_LAG * d
            pl.when((i >= 0) & (i < n_key))(functools.partial(hop, d, i))
        return carry

    lax.fori_loop(0, 2 * n_key, step, 0)

    CB[...] = CF[...].astype(BF16)
    for dr, dc in around:
        pl.when(inside(dr, dc))(lambda dr=dr, dc=dc: copy_h(dr, dc).start())
    for dr, dc in around:
        pl.when(inside(-dr, -dc))(lambda dr=dr, dc=dc: copy_h(dr, dc).wait_recv())

    halo = HB[...].astype(F32)
    place = lax.broadcasted_iota(jnp.int32, (pitch - width, halo.shape[-1]), 0)
    for b in range(height + 2):
        dr, row = (0, height - 1) if b == 0 else (2, 0) if b == height + 1 else (1, b - 1)
        left, right = halo[0, dr, row : row + 1], halo[1, dr, row : row + 1]
        both = jnp.where(place == 0, right, jnp.where(place == 1, left, 0.0))
        PQ[b, pl.ds(width, pitch - width)] = both.astype(BF16)

    def propagate(g, carry):
        own = PQ[pl.ds(g * GROUP + 1, GROUP), pl.ds(0, width)].reshape(GROUP * width, -1)
        beside = PQ[pl.ds(g * GROUP, GROUP + 2)].reshape(span, -1)
        weight = jnp.maximum(dot_t(own, beside), 0.0) * BAND[...]
        spread = dot_split(dot_split(weight * weight, beside), wp[...])
        blocks = GROUP * width // BLOCK
        PR[pl.ds(g * blocks, blocks)] = normalize(spread).astype(BF16).reshape(blocks, BLOCK, -1)
        return carry

    lax.fori_loop(0, height // GROUP, propagate, 0)

    for k in range(2 * n_key, n_key + HOP_LAG * (line - 1)):
        for d in range(1, line):
            if 0 <= k - HOP_LAG * d < n_key:
                hop(d, k - HOP_LAG * d)
    for i in range(n_key):
        copy_p(i).wait_recv()
        for q in range(line):
            copy_s(q, i, 1 - lane).wait_recv()

    key_px = lax.broadcasted_iota(jnp.int32, (BLOCK, BLOCK), 0)
    px = lax.broadcasted_iota(jnp.int32, (BLOCK, BLOCK), 1)
    line_of = px // width
    mirror = jnp.where(key_px == line_of * width + width - 1 - (px - line_of * width), INV_SHARP, 0.0).astype(F32)
    lines_per_block = BLOCK // width
    for b in range(per_tile):
        query = PR[b]
        total = jnp.zeros((1, BLOCK), F32)
        for n in range(shard.shape[-1]):
            negatives = KG[shard[0, 0, b, n], block[0, 0, b, n]]
            total += jnp.sum(jnp.exp(dot_t(negatives, query) * INV_SHARP), axis=0, keepdims=True)
        positive = jnp.sum(dot_t(PK[b], query) * mirror, axis=0, keepdims=True)
        loss = jnp.log(jnp.exp(positive) + total) - positive
        for row in range(lines_per_block):
            at = b * lines_per_block + row
            out[at : at + 1, :] = (
                valid[at : at + 1, :].astype(F32) * loss[:, row * width : (row + 1) * width]
            )

    for i in range(n_key):
        copy_p(i).wait_send()
    for dr, dc in around:
        pl.when(inside(dr, dc))(lambda dr=dr, dc=dc: copy_h(dr, dc).wait_send())

    def drain(q, carry):
        for i in range(n_key):
            copy_s(q, i, lane).wait_send()
            pl.when((q <= p) & (p < line - 1))(lambda i=i: copy_z(q, i, True).wait_send())
            pl.when((q >= p) & (p > 0))(lambda i=i: copy_z(q, i, False).wait_send())
        return carry

    lax.fori_loop(0, line, drain, 0)


def per_device(n_rows, n_cols, fq, fk, wh, wo, wp, valid, shard, block):
    height, width, channels = fq.shape
    pixels, wide, hid = height * width, wo.shape[1], wh.shape[1]
    n_key, per_tile, line = pixels // CHUNK, pixels // BLOCK, n_rows // 2
    pitch = width + 16
    any_space, vmem = pl.BlockSpec(memory_space=pl.ANY), pl.BlockSpec(memory_space=pltpu.VMEM)
    smem = pl.BlockSpec(memory_space=pltpu.SMEM)
    dma = pltpu.SemaphoreType.DMA
    return pl.pallas_call(
        functools.partial(kernel, n_rows, n_cols),
        out_shape=jax.ShapeDtypeStruct((height, width), F32),
        in_specs=[any_space] * 4 + [vmem, vmem, smem, smem],
        out_specs=vmem,
        scratch_shapes=[
            pltpu.VMEM((2 * n_key, CHUNK, channels), BF16),
            pltpu.VMEM((channels, hid), BF16),
            pltpu.VMEM((hid, wide), BF16),
            pltpu.VMEM((n_rows, per_tile, BLOCK, wide), BF16),
            pltpu.VMEM((per_tile, BLOCK, wide), BF16),
            pltpu.VMEM((height + 2, pitch, wide), BF16),
            pltpu.VMEM((2, height, wide), F32),
            pltpu.VMEM((2, height, wide), BF16),
            pltpu.VMEM((2, 3, height, wide), BF16),
            pltpu.VMEM((GROUP * width, (GROUP + 2) * pitch), F32),
            pltpu.VMEM((per_tile, BLOCK, wide), BF16),
            dma((2 * n_key,)),
            dma((2,)),
            dma((line, n_key)),
            dma((line, n_key)),
            dma((line, n_key)),
            dma((line, n_key)),
            dma((line, n_key)),
            dma((n_key,)),
            dma((n_key,)),
            dma((9,)),
            dma((9,)),
        ],
        compiler_params=pltpu.CompilerParams(
            collective_id=0, has_side_effects=True, vmem_limit_bytes=56 * 2**20
        ),
    )(fq.reshape(pixels, channels), fk.reshape(pixels, channels), wh, wo, wp, valid, shard, block)


def solution(mesh):
    tiles, heads = P("rows", "cols"), P("rows", "cols", None, None)
    return jax.shard_map(
        functools.partial(per_device, mesh.shape["rows"], mesh.shape["cols"]),
        mesh=mesh,
        in_specs=(P("rows", "cols", None), P("rows", "cols", None), P(), P(), P(), tiles, heads, heads),
        out_specs=tiles,
        check_vma=False,
    )
```

```python
import functools

import jax
import jax.numpy as jnp
from jax import lax
from jax.experimental import pallas as pl
from jax.experimental.pallas import tpu as pltpu
from jax.sharding import PartitionSpec as P

EPS = 1e-06
INV_SHARP = 10.0
CHUNK = 256
HOP_LAG = 3
GROUP = 4
BLOCK = 128
F32, BF16 = jnp.float32, jnp.bfloat16
MESH = pl.DeviceIdType.MESH


def normalize(v):
    return v * lax.rsqrt(jnp.sum(v * v, axis=-1, keepdims=True) + EPS)


def dot_t(a, b):
    return lax.dot_general(a, b, (((1,), (1,)), ((), ())), preferred_element_type=F32)


def dot_split(a, b):
    high = a.astype(BF16)
    low = (a - high.astype(F32)).astype(BF16)
    return jnp.dot(high, b, preferred_element_type=F32) + jnp.dot(
        low, b, preferred_element_type=F32
    )


def kernel(
    n_rows, n_cols,
    fq, fk, wh, wo, wp, valid, shard, block, out,
    X, WH, WO, KG, PK, PQ, CF, CB, HB, BAND, PR,
    load, load_w, zr, send_r, send_l, send_s, recv_s, part_s, part_r, halo_s, halo_r,
):
    r, c = lax.axis_index("rows"), lax.axis_index("cols")
    lane, p = lax.rem(r, 2), r // 2
    line = n_rows // 2
    sister = r + 1 - 2 * lane
    height, width = valid.shape
    pixels, per_tile = height * width, height * width // BLOCK
    n_key = pixels // CHUNK
    img = CHUNK // width
    per_chunk = CHUNK // BLOCK
    pitch = PQ.shape[1]

    loads = [pltpu.make_async_copy(wh, WH, load_w.at[0]), pltpu.make_async_copy(wo, WO, load_w.at[1])]
    for k in range(2 * n_key):
        source = fk if k < n_key else fq
        loads.append(
            pltpu.make_async_copy(
                source.at[pl.ds((k % n_key) * CHUNK, CHUNK)], X.at[k], load.at[k]
            )
        )
    for k in (2, 0, 1, *range(3, len(loads))):
        loads[k].start()

    HB[...] = jnp.zeros(HB.shape, BF16)
    PQ[...] = jnp.zeros(PQ.shape, BF16)

    span = (GROUP + 2) * pitch
    shape = (GROUP, width, span)
    a = lax.broadcasted_iota(jnp.int32, shape, 0)
    w = lax.broadcasted_iota(jnp.int32, shape, 1)
    t = lax.broadcasted_iota(jnp.int32, shape, 2)
    down = t // pitch
    j = t - down * pitch
    near = ((j < width) & (j - w <= 1) & (w - j <= 1)) | ((j == width) & (w == width - 1)) | ((j == width + 1) & (w == 0))
    near = near & (down >= a) & (down <= a + 2)
    BAND[...] = jnp.where(near, 1.0, 0.0).astype(F32).reshape(BAND.shape)

    around = [(dr, dc) for dr in (-1, 0, 1) for dc in (-1, 0, 1) if (dr, dc) != (0, 0)]

    def inside(dr, dc):
        return (r + dr >= 0) & (r + dr < n_rows) & (c + dc >= 0) & (c + dc < n_cols)

    barrier = pltpu.get_barrier_semaphore()

    def greet(target):
        pl.semaphore_signal(barrier, inc=1, device_id=target, device_id_type=MESH)

    mirrored = (r, n_cols - 1 - c)
    friends = [(True, (sister, c)), (True, mirrored), (p > 0, (r - 2, c)), (p < line - 1, (r + 2, c))]
    friends += [(inside(dr, dc), (r + dr, c + dc)) for dr, dc in around]
    for there, target in friends:
        if there is True:
            greet(target)
        else:
            pl.when(there)(functools.partial(greet, target))
    met = sum(1 if there is True else there.astype(jnp.int32) for there, _ in friends)
    pl.semaphore_wait(barrier, met)

    def keys_of(q, own, i):
        return KG.at[2 * q + own, pl.ds(i * per_chunk, per_chunk)]

    def copy_z(q, i, right):
        ref = keys_of(q, lane, i)
        return pltpu.make_async_remote_copy(
            src_ref=ref, dst_ref=ref,
            send_sem=(send_r if right else send_l).at[q, i], recv_sem=zr.at[q, i],
            device_id=(r + 2 if right else r - 2, c), device_id_type=MESH,
        )

    def copy_s(q, i, own):
        ref = keys_of(q, own, i)
        return pltpu.make_async_remote_copy(
            src_ref=ref, dst_ref=ref,
            send_sem=send_s.at[q, i], recv_sem=recv_s.at[q, i],
            device_id=(sister, c), device_id_type=MESH,
        )

    def copy_p(i):
        return pltpu.make_async_remote_copy(
            src_ref=keys_of(p, lane, i), dst_ref=PK.at[pl.ds(i * per_chunk, per_chunk)],
            send_sem=part_s.at[i], recv_sem=part_r.at[i],
            device_id=mirrored, device_id_type=MESH,
        )

    def copy_h(dr, dc):
        e = (dr + 1) * 3 + dc + 1
        if dc == 0:
            src = PQ.at[1 if dr < 0 else height, pl.ds(0, width)]
            dst = PQ.at[height + 1 if dr < 0 else 0, pl.ds(0, width)]
        else:
            side = 1 if dc > 0 else 0
            src, dst = CB.at[side], HB.at[1 - side, 1 - dr]
        return pltpu.make_async_remote_copy(
            src_ref=src, dst_ref=dst, send_sem=halo_s.at[e], recv_sem=halo_r.at[e],
            device_id=(r + dr, c + dc), device_id_type=MESH,
        )

    def hop(d, i):
        @pl.when(p - d >= 0)
        def _():
            q = p - d
            copy_z(q, i, True).wait_recv()
            pl.when(p < line - 1)(lambda: copy_z(q, i, True).start())
            copy_s(q, i, lane).start()

        @pl.when(p + d < line)
        def _():
            q = p + d
            copy_z(q, i, False).wait_recv()
            pl.when(p > 0)(lambda: copy_z(q, i, False).start())
            copy_s(q, i, lane).start()

    loads[0].wait()
    loads[1].wait()

    def step(k, carry):
        pltpu.make_async_copy(fk.at[pl.ds(0, CHUNK)], X.at[k], load.at[k]).wait()
        hidden = jnp.maximum(jnp.dot(X[k], WH[...], preferred_element_type=F32), 0.0)
        embedded = normalize(jnp.dot(hidden.astype(BF16), WO[...], preferred_element_type=F32))

        @pl.when(k < n_key)
        def _():
            KG[r, pl.ds(k * per_chunk, per_chunk)] = embedded.astype(BF16).reshape(per_chunk, BLOCK, -1)
            pl.when(p < line - 1)(lambda: copy_z(p, k, True).start())
            pl.when(p > 0)(lambda: copy_z(p, k, False).start())
            copy_s(p, k, lane).start()
            copy_p(k).start()

        @pl.when(k >= n_key)
        def _():
            first = (k - n_key) * img
            lines = embedded.reshape(img, width, -1)
            PQ[pl.ds(first + 1, img), pl.ds(0, width)] = lines.astype(BF16)
            for row in range(img):
                CF[0, pl.ds(first + row, 1)] = lines[row, 0:1]
                CF[1, pl.ds(first + row, 1)] = lines[row, width - 1 : width]

        for d in range(1, line):
            i = k - HOP_LAG * d
            pl.when((i >= 0) & (i < n_key))(functools.partial(hop, d, i))
        return carry

    lax.fori_loop(0, 2 * n_key, step, 0)

    CB[...] = CF[...].astype(BF16)
    for dr, dc in around:
        pl.when(inside(dr, dc))(lambda dr=dr, dc=dc: copy_h(dr, dc).start())
    for dr, dc in around:
        pl.when(inside(-dr, -dc))(lambda dr=dr, dc=dc: copy_h(dr, dc).wait_recv())

    halo = HB[...].astype(F32)
    place = lax.broadcasted_iota(jnp.int32, (pitch - width, halo.shape[-1]), 0)
    for b in range(height + 2):
        dr, row = (0, height - 1) if b == 0 else (2, 0) if b == height + 1 else (1, b - 1)
        left, right = halo[0, dr, row : row + 1], halo[1, dr, row : row + 1]
        both = jnp.where(place == 0, right, jnp.where(place == 1, left, 0.0))
        PQ[b, pl.ds(width, pitch - width)] = both.astype(BF16)

    def propagate(g, carry):
        own = PQ[pl.ds(g * GROUP + 1, GROUP), pl.ds(0, width)].reshape(GROUP * width, -1)
        beside = PQ[pl.ds(g * GROUP, GROUP + 2)].reshape(span, -1)
        weight = jnp.maximum(dot_t(own, beside), 0.0) * BAND[...]
        spread = dot_split(dot_split(weight * weight, beside), wp[...])
        blocks = GROUP * width // BLOCK
        PR[pl.ds(g * blocks, blocks)] = normalize(spread).astype(BF16).reshape(blocks, BLOCK, -1)
        return carry

    lax.fori_loop(0, height // GROUP, propagate, 0)

    for k in range(2 * n_key, n_key + HOP_LAG * (line - 1)):
        for d in range(1, line):
            if 0 <= k - HOP_LAG * d < n_key:
                hop(d, k - HOP_LAG * d)
    for i in range(n_key):
        copy_p(i).wait_recv()
        for q in range(line):
            copy_s(q, i, 1 - lane).wait_recv()

    key_px = lax.broadcasted_iota(jnp.int32, (BLOCK, BLOCK), 0)
    px = lax.broadcasted_iota(jnp.int32, (BLOCK, BLOCK), 1)
    line_of = px // width
    mirror = jnp.where(key_px == line_of * width + width - 1 - (px - line_of * width), INV_SHARP, 0.0).astype(F32)
    lines_per_block = BLOCK // width
    for b in range(per_tile):
        query = PR[b]
        total = jnp.zeros((1, BLOCK), F32)
        for n in range(shard.shape[0]):
            negatives = KG[shard[n, b], block[n, b]]
            total += jnp.sum(jnp.exp(dot_t(negatives, query) * INV_SHARP), axis=0, keepdims=True)
        positive = jnp.sum(dot_t(PK[b], query) * mirror, axis=0, keepdims=True)
        loss = jnp.log(jnp.exp(positive) + total) - positive
        for row in range(lines_per_block):
            at = b * lines_per_block + row
            out[at : at + 1, :] = (
                valid[at : at + 1, :].astype(F32) * loss[:, row * width : (row + 1) * width]
            )

    for i in range(n_key):
        copy_p(i).wait_send()
    for dr, dc in around:
        pl.when(inside(dr, dc))(lambda dr=dr, dc=dc: copy_h(dr, dc).wait_send())

    def drain(q, carry):
        for i in range(n_key):
            copy_s(q, i, lane).wait_send()
            pl.when((q <= p) & (p < line - 1))(lambda i=i: copy_z(q, i, True).wait_send())
            pl.when((q >= p) & (p > 0))(lambda i=i: copy_z(q, i, False).wait_send())
        return carry

    lax.fori_loop(0, line, drain, 0)


def per_device(n_rows, n_cols, fq, fk, wh, wo, wp, valid, shard, block):
    height, width, channels = fq.shape
    pixels, wide, hid = height * width, wo.shape[1], wh.shape[1]
    n_key, per_tile, line = pixels // CHUNK, pixels // BLOCK, n_rows // 2
    pitch = width + 16
    any_space, vmem = pl.BlockSpec(memory_space=pl.ANY), pl.BlockSpec(memory_space=pltpu.VMEM)
    smem = pl.BlockSpec(memory_space=pltpu.SMEM)
    dma = pltpu.SemaphoreType.DMA
    return pl.pallas_call(
        functools.partial(kernel, n_rows, n_cols),
        out_shape=jax.ShapeDtypeStruct((height, width), F32),
        in_specs=[any_space] * 4 + [vmem, vmem, smem, smem],
        out_specs=vmem,
        scratch_shapes=[
            pltpu.VMEM((2 * n_key, CHUNK, channels), BF16),
            pltpu.VMEM((channels, hid), BF16),
            pltpu.VMEM((hid, wide), BF16),
            pltpu.VMEM((n_rows, per_tile, BLOCK, wide), BF16),
            pltpu.VMEM((per_tile, BLOCK, wide), BF16),
            pltpu.VMEM((height + 2, pitch, wide), BF16),
            pltpu.VMEM((2, height, wide), F32),
            pltpu.VMEM((2, height, wide), BF16),
            pltpu.VMEM((2, 3, height, wide), BF16),
            pltpu.VMEM((GROUP * width, (GROUP + 2) * pitch), F32),
            pltpu.VMEM((per_tile, BLOCK, wide), BF16),
            dma((2 * n_key,)),
            dma((2,)),
            dma((line, n_key)),
            dma((line, n_key)),
            dma((line, n_key)),
            dma((line, n_key)),
            dma((line, n_key)),
            dma((n_key,)),
            dma((n_key,)),
            dma((9,)),
            dma((9,)),
        ],
        compiler_params=pltpu.CompilerParams(
            collective_id=0, has_side_effects=True, vmem_limit_bytes=56 * 2**20
        ),
    )(fq.reshape(pixels, channels), fk.reshape(pixels, channels), wh, wo, wp, valid, jnp.swapaxes(shard, 2, 3).reshape(-1, per_tile), jnp.swapaxes(block, 2, 3).reshape(-1, per_tile))


def solution(mesh):
    tiles, heads = P("rows", "cols"), P("rows", "cols", None, None)
    return jax.shard_map(
        functools.partial(per_device, mesh.shape["rows"], mesh.shape["cols"]),
        mesh=mesh,
        in_specs=(P("rows", "cols", None), P("rows", "cols", None), P(), P(), P(), tiles, heads, heads),
        out_specs=tiles,
        check_vma=False,
    )
```
